32 devices in a mesh: sec: 2 (over y), seq: 4 (over x, core), trk: 4 (over z).
Axes of the slice: x: 2, y: 2, z: 4, core: 2. Of those that a mesh axis runs over, the one named last changes fastest.
Arguments:
- tokens: bfloat16 [8, 256, 1536], P('sec', 'seq'), may hold values from -6 to 6
- norm_gain: bfloat16 [1536], replicated, may hold values from 0.25 to 1.75
- dilated_conv_weight: bfloat16 [1536, 3, 1536], P(None, None, 'trk'), may hold values from -0.09375 to 0.09375
- head_weight: bfloat16 [1536, 4, 40, 128], P(None, 'trk'), may hold values from -0.15625 to 0.15625
- targets: bfloat16 [8, 256, 4, 40, 128], P('sec', 'seq', 'trk'), may hold values from 0 to 2
- owner_tiles: int32 [4, 40], P('trk'), may hold values from -1 to 80, as said below
- species: int32 [8], P('sec'), may hold values from 0 to 1, as said below
Outputs:
- conv_grad: float32 [1536, 3, 1536], P(('sec', 'seq'), None, 'trk')
- head_grad: float32 [1536, 4, 40, 128], P(('sec', 'seq'), 'trk')
The draws below stay inside these ranges and needn't reach their ends.
Inputs may be any that keep to these rules, and one draw needn't show every extreme that they name: `owner_tiles`: each of the 81 tiles (human tiles 0 to 59, then the mouse tiles) stands in exactly one slot of one owner; -1 marks an empty slot; in every draw one owner has all 40 slots filled. `species`: 0 is human, 1 is mouse; exactly half of the samples are mouse.
All inputs are finite; a program needn't handle non-finite values.
Results may differ from the reference program's by a relative error of at most 0.0023.
Values may be sent and summed in bfloat16 or wider, within the bound.
A program may use at most 192 MiB of HBM per device.

```python
import math
import jax
import jax.numpy as jnp
from jax import lax

C = 1536
HTRACKS = 7611
MTRACKS = 2608
DILATION_BINS = 16
TAPS = 3
HTILES = 60
TILES = 81
SLOTS = 40
OWNERS = 4
SAMPLES = 8
SEQUENCE_BINS = 256
N_TRK = 4


def draw_owner_tiles(key, part):
    key_perm = jax.random.fold_in(key, 11)
    key_full = jax.random.fold_in(key, 12)
    key_place = jax.random.fold_in(key, 13)
    tile_order = jax.random.permutation(key_perm, TILES).astype(jnp.int32)
    full_owner = jax.random.randint(key_full, (), 0, N_TRK).astype(jnp.int32)
    other_slots = (N_TRK - 1) * SLOTS
    placing = jax.random.permutation(key_place, max(other_slots, 1)).astype(jnp.int32)
    others = jnp.full((max(other_slots, 1),), -1, jnp.int32)
    others = others.at[placing[:TILES - SLOTS]].set(tile_order[SLOTS:])
    others = others[:other_slots].reshape(N_TRK - 1, SLOTS)
    owner_rows = jnp.arange(N_TRK, dtype=jnp.int32)
    other_index = jnp.clip(jnp.where(owner_rows < full_owner, owner_rows, owner_rows - 1), 0, max(N_TRK - 2, 0))
    picked = jnp.take(others, other_index, axis=0)
    return jnp.where((owner_rows == full_owner)[:, None], tile_order[:SLOTS][None, :], picked).astype(jnp.int32)


def draw_species(key, part):
    order = jax.random.permutation(jax.random.fold_in(key, 21), SAMPLES).astype(jnp.int32)
    return (order % 2).astype(jnp.int32)


def level_of(stream_key, extent, split, least, top_value):
    factor_of = 1.0
    for dim, parts in split:
        draws = jax.random.uniform(jax.random.fold_in(jax.random.fold_in(stream_key, 6), dim), (parts,), jnp.float32, least / len(split), top_value / len(split))
        factor_of = factor_of * jnp.repeat(jnp.exp(draws), extent[dim] // parts).reshape((-1,) + (1,) * (len(extent) - 1 - dim))
    return factor_of


def centred(stream_key, extent, scale, bound, cuts=(), kind=jnp.bfloat16):
    array = scale * jax.random.normal(stream_key, extent, jnp.float32)
    if cuts:
        array = array * level_of(stream_key, extent, cuts, -0.22, 0.18)
    return jnp.clip(array, -bound, bound).astype(kind)


def setup_inputs(seed: int = 0) -> dict:
    streams_of = jax.random.split(jax.random.key(seed), 8)
    return {
        "tokens": centred(streams_of[0], (SAMPLES, SEQUENCE_BINS, C), 1.0, 6.0, ((0, 2), (1, 4))),
        "norm_gain": jnp.clip(1.0 + 0.15 * jax.random.normal(streams_of[1], (C,), jnp.float32), 0.25, 1.75).astype(jnp.bfloat16),
        "dilated_conv_weight": centred(streams_of[2], (C, TAPS, C), (TAPS * C) ** -0.5, 0.09375, ((2, 4),)),
        "head_weight": centred(streams_of[3], (C, OWNERS, SLOTS, 128), C ** -0.5, 0.15625, ((1, 4),)),
        "targets": jnp.clip(2.0 * jax.random.uniform(streams_of[4], (SAMPLES, SEQUENCE_BINS, OWNERS, SLOTS, 128), jnp.float32) ** level_of(streams_of[4], (SAMPLES, SEQUENCE_BINS, OWNERS, SLOTS, 128), ((0, 2), (1, 4), (2, 4)), -0.2, 0.2), 0.0, 2.0).astype(jnp.bfloat16),
        "owner_tiles": draw_owner_tiles(jax.random.fold_in(streams_of[7], 71), 0),
        "species": draw_species(jax.random.fold_in(streams_of[7], 71), 0),
    }


def contracted_rows(left, right):
    return lax.dot_general(left, right, (((0,), (0,)), ((), ())), preferred_element_type=jnp.float32)

def reference(tokens, norm_gain, dilated_conv_weight, head_weight, targets, owner_tiles, species):
    inputs = tokens.astype(jnp.float32)
    mean_sq = lax.optimization_barrier(jnp.mean(inputs * inputs, axis=-1, keepdims=True))
    normed = inputs * lax.rsqrt(mean_sq + 1e-06) * norm_gain.astype(jnp.float32)
    hidden_state = jax.nn.gelu(normed).astype(jnp.bfloat16)
    padded_input = jnp.pad(hidden_state, ((0, 0), (DILATION_BINS, DILATION_BINS), (0, 0)))
    tap_count = dilated_conv_weight.shape[1]
    mixed_list = []
    for sample_input in range(SAMPLES):
        convolution_output = jnp.zeros((SEQUENCE_BINS, C), jnp.float32)
        for kernel_tap_index in range(tap_count):
            convolution_output = convolution_output + jnp.dot(padded_input[sample_input, kernel_tap_index * DILATION_BINS:kernel_tap_index * DILATION_BINS + SEQUENCE_BINS], dilated_conv_weight[:, kernel_tap_index, :], preferred_element_type=jnp.float32)
        mixed_list.append((inputs[sample_input] + convolution_output).astype(jnp.bfloat16))
    mixed_all = jnp.stack(mixed_list)
    grad_scale = 1.0 / math.sqrt(SAMPLES * SEQUENCE_BINS)
    lane_ids = jnp.arange(128, dtype=jnp.int32)

    def owner_step(back_sum, owner_index):
        weights_owner = lax.dynamic_index_in_dim(head_weight, owner_index, 1, keepdims=False)
        tiles_owner = lax.dynamic_index_in_dim(owner_tiles, owner_index, 0, keepdims=False).astype(jnp.int32)
        targets_owner = lax.dynamic_index_in_dim(targets, owner_index, 2, keepdims=False)
        is_mouse = tiles_owner >= HTILES
        within = jnp.where(is_mouse, tiles_owner - HTILES, tiles_owner)
        track_limit = jnp.where(is_mouse, MTRACKS, HTRACKS).astype(jnp.int32)
        lane_mask = (within[:, None] * 128 + lane_ids[None, :] < track_limit[:, None]).astype(jnp.float32)
        grads_owner = jnp.zeros((C, SLOTS, 128), jnp.float32)
        new_back = []
        for sample_input in range(SAMPLES):
            active_int = ((tiles_owner >= 0) & (is_mouse == (species[sample_input] == 1))).astype(jnp.int32)
            slot_order = jnp.argsort(1 - active_int, stable=True).astype(jnp.int32)
            live_count = jnp.sum(active_int).astype(jnp.int32)
            mixed_here = mixed_all[sample_input]
            target_here = targets_owner[sample_input]

            def slot_step(position, loop_state):
                grads_now, back_now = loop_state
                slot_index = slot_order[position]
                column_w = lax.dynamic_index_in_dim(weights_owner, slot_index, 1, keepdims=False)
                logits = jnp.dot(mixed_here, column_w, preferred_element_type=jnp.float32)
                target_cols = lax.dynamic_index_in_dim(target_here, slot_index, 1, keepdims=False).astype(jnp.float32)
                mask_row = lax.dynamic_index_in_dim(lane_mask, slot_index, 0, keepdims=False)
                delta_f = grad_scale * (jax.nn.softplus(logits) - target_cols) * jax.nn.sigmoid(logits) * mask_row[None, :]
                delta_b = delta_f.astype(jnp.bfloat16)
                grads_now = grads_now.at[:, slot_index, :].add(contracted_rows(mixed_here, delta_b))
                back_now = back_now + lax.dot_general(delta_b, column_w, (((1,), (1,)), ((), ())), preferred_element_type=jnp.float32)
                return (grads_now, back_now)
            grads_owner, back_sample = lax.fori_loop(0, live_count, slot_step, (grads_owner, back_sum[sample_input]))
            new_back.append(back_sample)
        return (jnp.stack(new_back), grads_owner)
    back_sum, grads_all = lax.scan(owner_step, jnp.zeros((SAMPLES, SEQUENCE_BINS, C), jnp.float32), jnp.arange(OWNERS, dtype=jnp.int32))
    backward_bias = back_sum.astype(jnp.bfloat16)
    per_tap = []
    for kernel_tap_index in range(tap_count):
        running_total = jnp.zeros((C, C), jnp.float32)
        for sample_input in range(SAMPLES):
            running_total = running_total + contracted_rows(padded_input[sample_input, kernel_tap_index * DILATION_BINS:kernel_tap_index * DILATION_BINS + SEQUENCE_BINS], backward_bias[sample_input])
        per_tap.append(running_total)
    conv_grad = jnp.stack(per_tap, axis=1)
    total_sq = jnp.sum(grads_all * grads_all)
    entries = C * OWNERS * SLOTS * 128
    factor = jnp.minimum(1.0, 0.1 * lax.rsqrt(total_sq / entries + 1e-06))
    head_grad = jnp.transpose(grads_all * factor, (1, 0, 2, 3))
    return (conv_grad, head_grad)
```

```python
import math

import jax
import jax.numpy as jnp
from jax import lax
from jax.sharding import PartitionSpec as P

HTRACKS = 7611
MTRACKS = 2608
DILATION_BINS = 16
HTILES = 60
GRAD_CLIP = 0.1
SEND = jnp.float32


def padded(cells, axis, dim, width):
    count = lax.axis_size(axis)
    ends = count - 1
    head = lax.slice_in_dim(cells, 0, width, axis=dim)
    tail = lax.slice_in_dim(cells, cells.shape[dim] - width, cells.shape[dim], axis=dim)
    return jnp.concatenate(
        [
            lax.ppermute(tail, axis, [(i, (i + 1) % count) for i in range(ends)]),
            cells,
            lax.ppermute(head, axis, [((i + 1) % count, i) for i in range(ends)]),
        ],
        axis=dim,
    )


def live_mask(owner_tiles, species, lane_count):
    tiles = owner_tiles[0]
    is_mouse = tiles >= HTILES
    within = jnp.where(is_mouse, tiles - HTILES, tiles)
    limit = jnp.where(is_mouse, MTRACKS, HTRACKS).astype(jnp.int32)
    lanes = jnp.arange(lane_count, dtype=jnp.int32)
    valid = (within[:, None] * lane_count + lanes[None, :] < limit[:, None]) & (tiles >= 0)[:, None]
    live = is_mouse[None, :] == (species == 1)[:, None]
    return (live[:, :, None] & valid[None]).astype(jnp.float32)


def body(tokens, norm_gain, dilated_conv_weight, head_weight, targets, owner_tiles, species):
    samples, bins, width = tokens.shape
    taps = dilated_conv_weight.shape[1]
    out_share = dilated_conv_weight.shape[2]
    slots, lanes = head_weight.shape[2:]
    owners = lax.axis_size("trk")
    rows = samples * bins
    columns = slots * lanes

    inputs = tokens.astype(jnp.float32)
    mean_sq = jnp.mean(inputs * inputs, axis=-1, keepdims=True)
    normed = inputs * lax.rsqrt(mean_sq + 1e-06) * norm_gain.astype(jnp.float32)
    hidden = jax.nn.gelu(normed).astype(jnp.bfloat16)
    hidden = padded(hidden, "seq", 1, DILATION_BINS)
    shifted = [
        hidden[:, k * DILATION_BINS : k * DILATION_BINS + bins].reshape(rows, width)
        for k in range(taps)
    ]
    conv = sum(
        jnp.dot(shifted[k], dilated_conv_weight[:, k, :], preferred_element_type=jnp.float32)
        for k in range(taps)
    )
    own = lax.dynamic_slice_in_dim(tokens, lax.axis_index("trk") * out_share, out_share, 2)
    mixed_share = (own.reshape(rows, out_share).astype(jnp.float32) + conv).astype(jnp.bfloat16)
    gathered = lax.all_gather(mixed_share, "trk", axis=0)
    mixed = jnp.concatenate([gathered[g] for g in range(owners)], axis=-1)

    weights = head_weight.reshape(width, columns)
    mask = live_mask(owner_tiles, species, lanes).reshape(samples, 1, columns)
    grad_scale = 1.0 / math.sqrt(
        lax.axis_size("sec") * samples * lax.axis_size("seq") * bins
    )
    logits = jnp.dot(mixed, weights, preferred_element_type=jnp.float32)
    decay = jnp.exp(-jnp.abs(logits))
    softplus = jnp.maximum(logits, 0.0) + jnp.log(1.0 + decay)
    sigmoid = jnp.where(logits >= 0, 1.0, decay) / (1.0 + decay)
    wanted = targets.reshape(rows, columns).astype(jnp.float32)
    spread = jnp.broadcast_to(mask * grad_scale, (samples, bins, columns)).reshape(rows, columns)
    delta = (spread * (softplus - wanted) * sigmoid).astype(jnp.bfloat16)

    raw = lax.dot_general(
        mixed, delta, (((0,), (0,)), ((), ())), preferred_element_type=jnp.float32
    ).astype(SEND)
    raw = lax.psum_scatter(raw, ("sec", "seq"), scatter_dimension=0, tiled=True)
    raw = raw.astype(jnp.float32)

    back = lax.dot_general(
        delta, weights, (((1,), (1,)), ((), ())), preferred_element_type=jnp.float32
    )
    back = jnp.stack([back[:, g * out_share : (g + 1) * out_share] for g in range(owners)])
    back = lax.psum_scatter(back, "trk", scatter_dimension=0, tiled=True)[0].astype(jnp.bfloat16)
    conv_part = jnp.concatenate(
        [
            lax.dot_general(
                shifted[k], back, (((0,), (0,)), ((), ())), preferred_element_type=jnp.float32
            )
            for k in range(taps)
        ],
        axis=1,
    ).astype(SEND)
    conv_grad = lax.psum_scatter(conv_part, ("sec", "seq"), scatter_dimension=0, tiled=True)
    conv_grad = conv_grad.astype(jnp.float32).reshape(-1, taps, out_share)

    total_sq = lax.psum(jnp.sum(raw * raw), ("sec", "seq", "trk"))
    entries = width * owners * columns
    factor = jnp.minimum(1.0, GRAD_CLIP * lax.rsqrt(total_sq / entries + 1e-06))
    head_grad = (raw * factor).reshape(-1, 1, slots, lanes)
    return conv_grad, head_grad


def solution(mesh):
    return jax.shard_map(
        body,
        mesh=mesh,
        in_specs=(
            P("sec", "seq", None),
            P(),
            P(None, None, "trk"),
            P(None, "trk", None, None),
            P("sec", "seq", "trk", None, None),
            P("trk", None),
            P("sec"),
        ),
        out_specs=(P(("sec", "seq"), None, "trk"), P(("sec", "seq"), "trk", None, None)),
        check_vma=False,
    )
```

```python
import math

import jax
import jax.numpy as jnp
from jax import lax
from jax.sharding import PartitionSpec as P

HTRACKS = 7611
MTRACKS = 2608
DILATION_BINS = 16
HTILES = 60
GRAD_CLIP = 0.1
SEND = jnp.bfloat16
CORES = 2


def padded(cells, axis, dim, width):
    count = lax.axis_size(axis)
    ends = count - 1
    head = lax.slice_in_dim(cells, 0, width, axis=dim)
    tail = lax.slice_in_dim(cells, cells.shape[dim] - width, cells.shape[dim], axis=dim)
    return jnp.concatenate(
        [
            lax.ppermute(tail, axis, [(i, (i + 1) % count) for i in range(ends)]),
            cells,
            lax.ppermute(head, axis, [((i + 1) % count, i) for i in range(ends)]),
        ],
        axis=dim,
    )


def live_mask(owner_tiles, species, lane_count):
    tiles = owner_tiles[0]
    is_mouse = tiles >= HTILES
    within = jnp.where(is_mouse, tiles - HTILES, tiles)
    limit = jnp.where(is_mouse, MTRACKS, HTRACKS).astype(jnp.int32)
    lanes = jnp.arange(lane_count, dtype=jnp.int32)
    valid = (within[:, None] * lane_count + lanes[None, :] < limit[:, None]) & (tiles >= 0)[:, None]
    live = is_mouse[None, :] == (species == 1)[:, None]
    return (live[:, :, None] & valid[None]).astype(jnp.float32)


def shift_seq(cells, offset):
    count = lax.axis_size("seq")
    return lax.ppermute(
        cells, "seq", [(i, (i + offset * CORES) % count) for i in range(count)]
    )


def shift_axis(cells, axis, offset):
    count = lax.axis_size(axis)
    return lax.ppermute(cells, axis, [(i, (i + offset) % count) for i in range(count)])


def from_mate(cells):
    return lax.ppermute(cells, "seq", [(i, i ^ 1) for i in range(lax.axis_size("seq"))])


def with_mate(cells):
    return jnp.concatenate([cells, from_mate(cells)], axis=0)


def core_columns(cells):
    groups = lax.axis_size("sec") * (lax.axis_size("seq") // CORES)
    split = cells.reshape(cells.shape[0], groups, CORES, -1)
    core = lax.rem(lax.axis_index("seq"), CORES)
    mine = lax.dynamic_index_in_dim(split, core, 2, keepdims=False)
    other = lax.dynamic_index_in_dim(split, 1 - core, 2, keepdims=False)
    both = jnp.concatenate([mine, from_mate(other)], axis=0)
    return both.reshape(both.shape[0], lax.axis_size("sec"), -1, both.shape[-1])


def reduced_product(left, right, chips_first):
    place = {
        1: (lax.axis_index("sec"), lax.axis_size("sec"), lambda c, k: shift_axis(c, "sec", k)),
        2: (lax.axis_index("seq") // CORES, lax.axis_size("seq") // CORES, shift_seq),
    }
    first, second = (2, 1) if chips_first else (1, 2)
    here, count, send = place[first]

    def product(index):
        part = lax.dynamic_index_in_dim(left, index, first, keepdims=False)
        out = lax.dot_general(
            part.reshape(part.shape[0], -1),
            right,
            (((0,), (0,)), ((), ())),
            preferred_element_type=jnp.float32,
        )
        return out.reshape(part.shape[1], part.shape[2], -1)

    arrived = [
        send(product(lax.rem(here + k, count)).astype(SEND), k) for k in range(1, count)
    ]
    total = product(here)
    for block in arrived:
        total = total + block.astype(jnp.float32)
    here, count, send = place[second]
    arrived = [
        send(
            lax.dynamic_index_in_dim(
                total, lax.rem(here + k, count), 0, keepdims=False
            ).astype(SEND),
            k,
        )
        for k in range(1, count)
    ]
    total = lax.dynamic_index_in_dim(total, here, 0, keepdims=False)
    for block in arrived:
        total = total + block.astype(jnp.float32)
    return total


def body(tokens, norm_gain, dilated_conv_weight, head_weight, targets, owner_tiles, species):
    samples, bins, width = tokens.shape
    taps = dilated_conv_weight.shape[1]
    out_share = dilated_conv_weight.shape[2]
    slots, lanes = head_weight.shape[2:]
    owners = lax.axis_size("trk")
    rows = samples * bins
    columns = slots * lanes

    inputs = tokens.astype(jnp.float32)
    mean_sq = jnp.mean(inputs * inputs, axis=-1, keepdims=True)
    normed = inputs * lax.rsqrt(mean_sq + 1e-06) * norm_gain.astype(jnp.float32)
    hidden = jax.nn.gelu(normed).astype(jnp.bfloat16)
    hidden = padded(hidden, "seq", 1, DILATION_BINS)
    shifted = [
        hidden[:, k * DILATION_BINS : k * DILATION_BINS + bins].reshape(rows, width)
        for k in range(taps)
    ]
    conv = sum(
        jnp.dot(shifted[k], dilated_conv_weight[:, k, :], preferred_element_type=jnp.float32)
        for k in range(taps)
    )
    own = lax.dynamic_slice_in_dim(tokens, lax.axis_index("trk") * out_share, out_share, 2)
    mixed_share = (own.reshape(rows, out_share).astype(jnp.float32) + conv).astype(jnp.bfloat16)
    gathered = lax.all_gather(mixed_share, "trk", axis=0)
    mixed = jnp.concatenate([gathered[g] for g in range(owners)], axis=-1)

    weights = head_weight.reshape(width, columns)
    mask = live_mask(owner_tiles, species, lanes).reshape(samples, 1, columns)
    grad_scale = 1.0 / math.sqrt(
        lax.axis_size("sec") * samples * lax.axis_size("seq") * bins
    )
    logits = jnp.dot(mixed, weights, preferred_element_type=jnp.float32)
    decay = jnp.exp(-jnp.abs(logits))
    softplus = jnp.maximum(logits, 0.0) + jnp.log(1.0 + decay)
    sigmoid = jnp.where(logits >= 0, 1.0, decay) / (1.0 + decay)
    wanted = targets.reshape(rows, columns).astype(jnp.float32)
    spread = jnp.broadcast_to(mask * grad_scale, (samples, bins, columns)).reshape(rows, columns)
    delta = (spread * (softplus - wanted) * sigmoid).astype(jnp.bfloat16)

    back = lax.dot_general(
        delta, weights, (((1,), (1,)), ((), ())), preferred_element_type=jnp.float32
    )
    back = jnp.stack([back[:, g * out_share : (g + 1) * out_share] for g in range(owners)])
    me = lax.axis_index("trk")
    arrived = [
        shift_axis(
            lax.dynamic_index_in_dim(back, lax.rem(me + k, owners), 0, keepdims=False).astype(SEND),
            "trk",
            k,
        )
        for k in range(1, owners)
    ]
    back = lax.dynamic_index_in_dim(back, me, 0, keepdims=False)
    for block in arrived:
        back = back + block.astype(jnp.float32)
    back = with_mate(back.astype(jnp.bfloat16))

    delta = with_mate(delta)
    left = core_columns(mixed)
    half = columns // 2
    raw = [
        reduced_product(left, delta[:, :half], True),
        reduced_product(left, delta[:, half:], False),
    ]
    conv_grad = jnp.stack(
        [
            reduced_product(core_columns(shifted[k]), back, k % 2 == 0)
            for k in range(taps)
        ],
        axis=1,
    )

    total_sq = lax.psum(sum(jnp.sum(r * r) for r in raw), ("sec", "seq", "trk"))
    entries = width * owners * columns
    factor = jnp.minimum(1.0, GRAD_CLIP * lax.rsqrt(total_sq / entries + 1e-06))
    head_grad = jnp.concatenate(
        [(r * factor).reshape(-1, 1, slots // 2, lanes) for r in raw], axis=2
    )
    return conv_grad, head_grad


def solution(mesh):
    return jax.shard_map(
        body,
        mesh=mesh,
        in_specs=(
            P("sec", "seq", None),
            P(),
            P(None, None, "trk"),
            P(None, "trk", None, None),
            P("sec", "seq", "trk", None, None),
            P("trk", None),
            P("sec"),
        ),
        out_specs=(P(("sec", "seq"), None, "trk"), P(("sec", "seq"), "trk", None, None)),
        check_vma=False,
    )
```

```python
import math

import jax
import jax.numpy as jnp
from jax import lax
from jax.sharding import PartitionSpec as P

HTRACKS = 7611
MTRACKS = 2608
DILATION_BINS = 16
HTILES = 60
GRAD_CLIP = 0.1
SEND = jnp.bfloat16
CORES = 2


def padded(cells, axis, dim, width):
    count = lax.axis_size(axis)
    ends = count - 1
    head = lax.slice_in_dim(cells, 0, width, axis=dim)
    tail = lax.slice_in_dim(cells, cells.shape[dim] - width, cells.shape[dim], axis=dim)
    return jnp.concatenate(
        [
            lax.ppermute(tail, axis, [(i, (i + 1) % count) for i in range(ends)]),
            cells,
            lax.ppermute(head, axis, [((i + 1) % count, i) for i in range(ends)]),
        ],
        axis=dim,
    )


def live_mask(owner_tiles, species, lane_count):
    tiles = owner_tiles[0]
    is_mouse = tiles >= HTILES
    within = jnp.where(is_mouse, tiles - HTILES, tiles)
    limit = jnp.where(is_mouse, MTRACKS, HTRACKS).astype(jnp.int32)
    lanes = jnp.arange(lane_count, dtype=jnp.int32)
    valid = (within[:, None] * lane_count + lanes[None, :] < limit[:, None]) & (tiles >= 0)[:, None]
    live = is_mouse[None, :] == (species == 1)[:, None]
    return (live[:, :, None] & valid[None]).astype(jnp.float32)


def shift_seq(cells, offset):
    count = lax.axis_size("seq")
    return lax.ppermute(
        cells, "seq", [(i, (i + offset * CORES) % count) for i in range(count)]
    )


def shift_axis(cells, axis, offset):
    count = lax.axis_size(axis)
    return lax.ppermute(cells, axis, [(i, (i + offset) % count) for i in range(count)])


def from_mate(cells):
    return lax.ppermute(cells, "seq", [(i, i ^ 1) for i in range(lax.axis_size("seq"))])


def with_mate(cells):
    return jnp.concatenate([cells, from_mate(cells)], axis=0)


def picked(cells, chips_first):
    width = cells.shape[-1]
    secs, chips = lax.axis_size("sec"), lax.axis_size("seq") // CORES
    size = width // (secs * chips * CORES)
    seq = lax.axis_index("seq")
    place = jnp.arange(width // CORES, dtype=jnp.int32)
    group = place // size
    if chips_first:
        sec = group % secs
        chip = (group // secs + seq // CORES) % chips
    else:
        chip = group % chips
        sec = (group // chips + lax.axis_index("sec")) % secs
    source = ((sec * chips + chip) * CORES + seq % CORES) * size + place % size
    choice = jnp.arange(width, dtype=jnp.int32)[:, None] == source[None, :]
    return jnp.dot(
        cells, choice.astype(cells.dtype), preferred_element_type=jnp.float32
    ).astype(cells.dtype)


def reduced_product(pairs, size, chips_first):
    place = (
        (lax.axis_index("sec"), lax.axis_size("sec"), lambda c, k: shift_axis(c, "sec", k)),
        (lax.axis_index("seq") // CORES, lax.axis_size("seq") // CORES, shift_seq),
    )
    first, second = (1, 0) if chips_first else (0, 1)
    here, count, send = place[first]
    inner = place[second][1]

    def product(k):
        outs = [
            lax.dot_general(
                left[:, k * inner * size : (k + 1) * inner * size],
                right,
                (((0,), (0,)), ((), ())),
                preferred_element_type=jnp.float32,
            )
            for left, right in pairs
        ]
        out = outs[0] if len(outs) == 1 else jnp.concatenate(outs, axis=1)
        return out.reshape(inner, size, -1)

    arrived = [send(product(k).astype(SEND), k) for k in range(1, count)]
    total = product(0)
    for block in arrived:
        total = total + block.astype(jnp.float32)
    here, count, send = place[second]
    arrived = [
        send(
            lax.dynamic_index_in_dim(
                total, lax.rem(here + k, count), 0, keepdims=False
            ).astype(SEND),
            k,
        )
        for k in range(1, count)
    ]
    total = lax.dynamic_index_in_dim(total, here, 0, keepdims=False)
    for block in arrived:
        total = total + block.astype(jnp.float32)
    return total


def body(tokens, norm_gain, dilated_conv_weight, head_weight, targets, owner_tiles, species):
    samples, bins, width = tokens.shape
    taps = dilated_conv_weight.shape[1]
    out_share = dilated_conv_weight.shape[2]
    slots, lanes = head_weight.shape[2:]
    owners = lax.axis_size("trk")
    rows = samples * bins
    columns = slots * lanes

    inputs = tokens.astype(jnp.float32)
    mean_sq = jnp.mean(inputs * inputs, axis=-1, keepdims=True)
    normed = inputs * lax.rsqrt(mean_sq + 1e-06) * norm_gain.astype(jnp.float32)
    hidden = jax.nn.gelu(normed).astype(jnp.bfloat16)
    hidden = padded(hidden, "seq", 1, DILATION_BINS)
    hidden_both = with_mate(hidden)
    shifted = [
        hidden[:, k * DILATION_BINS : k * DILATION_BINS + bins].reshape(rows, width)
        for k in range(taps)
    ]
    conv = sum(
        jnp.dot(shifted[k], dilated_conv_weight[:, k, :], preferred_element_type=jnp.float32)
        for k in range(taps)
    )
    own = lax.dynamic_slice_in_dim(tokens, lax.axis_index("trk") * out_share, out_share, 2)
    mixed_share = (own.reshape(rows, out_share).astype(jnp.float32) + conv).astype(jnp.bfloat16)
    gathered = lax.all_gather(mixed_share, "trk", axis=0)
    mixed = jnp.concatenate([gathered[g] for g in range(owners)], axis=-1)

    weights = head_weight.reshape(width, columns)
    mask = live_mask(owner_tiles, species, lanes).reshape(samples, 1, columns)
    grad_scale = 1.0 / math.sqrt(
        lax.axis_size("sec") * samples * lax.axis_size("seq") * bins
    )
    logits = jnp.dot(mixed, weights, preferred_element_type=jnp.float32)
    decay = jnp.exp(-jnp.abs(logits))
    softplus = jnp.maximum(logits, 0.0) + jnp.log(1.0 + decay)
    sigmoid = jnp.where(logits >= 0, 1.0, decay) / (1.0 + decay)
    wanted = targets.reshape(rows, columns).astype(jnp.float32)
    spread = jnp.broadcast_to(mask * grad_scale, (samples, bins, columns)).reshape(rows, columns)
    delta = (spread * (softplus - wanted) * sigmoid).astype(jnp.bfloat16)

    back = lax.dot_general(
        delta, weights, (((1,), (1,)), ((), ())), preferred_element_type=jnp.float32
    )
    back = jnp.stack([back[:, g * out_share : (g + 1) * out_share] for g in range(owners)])
    me = lax.axis_index("trk")
    arrived = [
        shift_axis(
            lax.dynamic_index_in_dim(back, lax.rem(me + k, owners), 0, keepdims=False).astype(SEND),
            "trk",
            k,
        )
        for k in range(1, owners)
    ]
    back = lax.dynamic_index_in_dim(back, me, 0, keepdims=False)
    for block in arrived:
        back = back + block.astype(jnp.float32)
    back = with_mate(back.astype(jnp.bfloat16))

    delta = with_mate(delta)
    both = with_mate(mixed)
    size = width // (lax.axis_size("sec") * lax.axis_size("seq"))
    half = columns // 2
    raw = [
        reduced_product([(picked(both, True), delta[:, :half])], size, True),
        reduced_product([(picked(both, False), delta[:, half:])], size, False),
    ]
    conv_parts = [None] * taps
    for chips_first in (True, False):
        chosen = [k for k in range(taps) if (k % 2 == 0) == chips_first]
        lefts = picked(hidden_both, chips_first)
        pairs = [
            (
                lefts[:, k * DILATION_BINS : k * DILATION_BINS + bins].reshape(
                    CORES * rows, -1
                ),
                back,
            )
            for k in chosen
        ]
        part = reduced_product(pairs, size, chips_first)
        for i, k in enumerate(chosen):
            conv_parts[k] = part[:, i * out_share : (i + 1) * out_share]
    conv_grad = jnp.stack(conv_parts, axis=1)

    total_sq = lax.psum(sum(jnp.sum(r * r) for r in raw), ("sec", "seq", "trk"))
    entries = width * owners * columns
    factor = jnp.minimum(1.0, GRAD_CLIP * lax.rsqrt(total_sq / entries + 1e-06))
    head_grad = jnp.concatenate(
        [(r * factor).reshape(-1, 1, slots // 2, lanes) for r in raw], axis=2
    )
    return conv_grad, head_grad


def solution(mesh):
    return jax.shard_map(
        body,
        mesh=mesh,
        in_specs=(
            P("sec", "seq", None),
            P(),
            P(None, None, "trk"),
            P(None, "trk", None, None),
            P("sec", "seq", "trk", None, None),
            P("trk", None),
            P("sec"),
        ),
        out_specs=(P(("sec", "seq"), None, "trk"), P(("sec", "seq"), "trk", None, None)),
        check_vma=False,
    )
```
